256 devices in a mesh: ctx: 64 (over z, y_lo, x), tp: 4 (over y_hi, core).
Axes of the slice: x: 4, y: 4 (y_hi: 2, y_lo: 2; y = y_hi * 2 + y_lo), z: 8, core: 2. Of those that a mesh axis runs over, the one named last changes fastest.
Arguments:
- queries: bfloat16 [16384, 8192], P('ctx', 'tp'), may hold values from -6 to 6
- key_proj: bfloat16 [16384, 8192], P('ctx', 'tp'), may hold values from -6 to 6
- values: bfloat16 [16384, 8192], P('ctx', 'tp'), may hold values from -6 to 6
- residues: float32 [16, 8192], P(None, 'tp'), may hold values from -0.4 to 0.4
- decay_rates: float32 [16, 8192], P(None, 'tp'), may hold values from 0 to 0.034, as said below
- skip_weight: float32 [8192], P('tp'), may hold values from 0.5 to 1.5
- stream: bfloat16 [16384, 8192], P('ctx', 'tp'), may hold values from -110 to 110
- norm_gain: float32 [8192], P('tp'), may hold values from 0.1 to 1.9
Outputs:
- new_stream: bfloat16 [16384, 8192], P('ctx', 'tp')
- normed: bfloat16 [16384, 8192], P('ctx', 'tp')
The draws below stay inside these ranges and needn't reach their ends.
Inputs may be any that keep to these rules, and one draw needn't show every extreme that they name: `decay_rates`: each mode's decay per position; all positive.
All inputs are finite; a program needn't handle non-finite values.
Results may differ from the reference program's by a relative error of at most 0.007.
Values may be sent and summed in bfloat16 or wider, within the bound.
No kernel may reach another device: no remote copies, remote signals or barrier semaphores. Data moves between devices by JAX's collectives and lax.ppermute only.
A program may use at most 128 MiB of HBM per device.

```python
import math
import jax
import jax.numpy as jnp
from jax import lax

D = 8192
MODES = 16
SEQ = 16384


def modal_rates(key, lowest, highest):
    fraction = jax.random.uniform(key, (MODES, D), jnp.float32)
    return jnp.exp(jnp.log(lowest) + fraction * (jnp.log(highest) - jnp.log(lowest)))


def draw_decay_rates(key, part):
    return modal_rates(key, 0.5 / SEQ, 1.0 / 30.0)


def draw_residues(key, part):
    decay = modal_rates(key, 0.5 / SEQ, 1.0 / 30.0)
    key = jax.random.fold_in(key, 7)
    base = 0.25 * jnp.clip(jax.random.normal(key, (MODES, D), jnp.float32), -6.0, 6.0)
    return base * jnp.sqrt(2.0 * decay)


def draw_stream(key, part):
    key = jax.random.fold_in(key, 5)
    key_cols, key_rows, key_base = jax.random.split(key, 3)
    ramp = jnp.arange(D, dtype=jnp.float32) / D
    spread = 10.0 ** jax.random.uniform(key_cols, (D,), jnp.float32)
    row_scale = 10.0 ** jax.random.uniform(key_rows, (SEQ, 1), jnp.float32, -0.5, 0.5)
    column_scale = 3.0 ** ramp * spread / 6.0
    base = jnp.clip(jax.random.normal(key_base, (SEQ, D), jnp.float32), -6.0, 6.0)
    return (base * row_scale * column_scale[None, :]).astype(jnp.bfloat16)


def steps_of(rng, shape, cuts, least, largest):
    def one(position, parts):
        draws = jax.random.uniform(jax.random.fold_in(jax.random.fold_in(rng, 6), position), (parts,), jnp.float32, least / len(cuts), largest / len(cuts))
        return jnp.repeat(jnp.exp(draws), shape[position] // parts).reshape((-1,) + (1,) * (len(shape) - position - 1))

    gain = one(*cuts[0])
    for cut in cuts[1:]:
        gain = gain * one(*cut)
    return gain


def centred(rng, extent, scale, most, cuts=(), held_as=jnp.bfloat16):
    values = scale * jax.random.normal(rng, extent, jnp.float32)
    if cuts:
        values = values * steps_of(rng, extent, cuts, -0.22, 0.18)
    return jnp.clip(values, -most, most).astype(held_as)


def setup_inputs(seed: int = 0) -> dict:
    splits = jax.random.split(jax.random.key(seed), 9)
    return {
        "queries": centred(splits[0], (SEQ, D), 1.0, 6.0, ((0, 64), (1, 4))),
        "key_proj": centred(splits[1], (SEQ, D), 1.0, 6.0, ((0, 64), (1, 4))),
        "values": centred(splits[2], (SEQ, D), 1.0, 6.0, ((0, 64), (1, 4))),
        "residues": draw_residues(jax.random.fold_in(splits[8], 71), 0),
        "decay_rates": draw_decay_rates(jax.random.fold_in(splits[8], 71), 0),
        "skip_weight": jnp.clip(0.5 + 1.0 * jax.random.uniform(splits[5], (D,), jnp.float32) ** steps_of(splits[5], (D,), ((0, 4),), -0.2, 0.2), 0.5, 1.5),
        "stream": draw_stream(jax.random.fold_in(splits[8], 71), 0),
        "norm_gain": jnp.clip(1.0 + 0.18 * jax.random.normal(splits[7], (D,), jnp.float32), 0.1, 1.9),
    }


epsilon = 1e-06

def reference(queries, key_proj, values, residues, decay_rates, skip_weight, stream, norm_gain):
    signal = (queries.astype(jnp.float32) * key_proj.astype(jnp.float32)).astype(jnp.bfloat16)
    widened = lax.optimization_barrier(signal).astype(jnp.float32)
    channel_group = math.gcd(D, 256)
    group_count = D // channel_group

    def split_groups(source, length):
        return source.reshape(length, group_count, channel_group).transpose(1, 0, 2)

    def conv_group(pieces):
        part_signal, part_decay, part_residue = pieces
        positions = jnp.arange(SEQ, dtype=jnp.float32)[:, None]
        kernel_taps = jnp.zeros((SEQ, channel_group), jnp.float32)
        for mode_index in range(MODES):
            kernel_taps = kernel_taps + part_residue[mode_index] * jnp.exp(-part_decay[mode_index] * positions)
        spectrum = jnp.fft.rfft(part_signal, n=2 * SEQ, axis=0) * jnp.fft.rfft(kernel_taps, n=2 * SEQ, axis=0)
        return jnp.fft.irfft(spectrum, n=2 * SEQ, axis=0)[:SEQ]
    convolved = lax.map(conv_group, (split_groups(widened, SEQ), split_groups(decay_rates, MODES), split_groups(residues, MODES)))
    convolved = convolved.transpose(1, 0, 2).reshape(SEQ, D)
    mixed = values.astype(jnp.float32) * (convolved + skip_weight[None, :] * widened)
    new_stream = (stream.astype(jnp.float32) + mixed).astype(jnp.bfloat16)
    restored = lax.optimization_barrier(new_stream).astype(jnp.float32)
    row_power = lax.optimization_barrier(jnp.mean(restored * restored, axis=1, keepdims=True))
    normed = (restored * lax.rsqrt(row_power + epsilon) * norm_gain[None, :]).astype(jnp.bfloat16)
    return (new_stream, normed)
```

```python
import functools

import jax
import jax.numpy as jnp
from jax import lax
from jax.experimental import pallas as pl
from jax.experimental.pallas import tpu as pltpu
from jax.sharding import PartitionSpec as P

epsilon = 1e-06
lanes = 128
sublanes = 8
piece_width = 512
vmem_bytes = 24 * 1024 * 1024


def at_group(group):
    return pl.ds(pl.multiple_of(group * lanes, lanes), lanes)


def spread(ref, mode, cols):
    return jnp.broadcast_to(ref[pl.ds(mode, 1), cols], (sublanes, lanes))


def tree_sum(parts):
    parts = list(parts)
    while len(parts) > 1:
        parts = [l + r for l, r in zip(parts[::2], parts[1::2])]
    return parts[0]


def state_kernel(
    span, q_hbm, k_hbm, v_hbm, x_hbm, decay_hbm, res_hbm, skip_hbm,
    total_ref, sent_ref, chunk_ref, sig_ref, v_ref, x_ref, decay_ref, res_ref, skip_ref,
    q_ref, k_ref, rows_ref, pair_sem, side_sem,
):
    modes = decay_ref.shape[0]
    rows, width = q_ref.shape
    pieces = width // piece_width
    pair = []
    first = pltpu.make_async_copy(decay_hbm, decay_ref, side_sem.at[0])
    first.start()
    for p in range(pieces):
        cols = pl.ds(p * piece_width, piece_width)
        for at, (src, dst) in enumerate(((q_hbm, q_ref), (k_hbm, k_ref))):
            pair.append(pltpu.make_async_copy(src.at[:, cols], dst.at[:, cols], pair_sem.at[at, p]))
            pair[-1].start()
    side = []
    for at, (src, dst) in enumerate(((v_hbm, v_ref), (x_hbm, x_ref), (res_hbm, res_ref), (skip_hbm, skip_ref))):
        side.append(pltpu.make_async_copy(src, dst, side_sem.at[at + 1]))
        side[-1].start()
    run = lax.broadcasted_iota(jnp.int32, (sublanes, lanes), 0)
    left = ((sublanes - 1 - run) * span).astype(jnp.float32)
    first.wait()
    for p in range(pieces):
        pair[2 * p].wait()
        pair[2 * p + 1].wait()

        @pl.loop(p * piece_width // lanes, (p + 1) * piece_width // lanes)
        def _(group):
            cols = at_group(group)
            product = q_ref[:, cols].astype(jnp.float32) * k_ref[:, cols].astype(jnp.float32)
            rows_ref[...] = product.astype(jnp.bfloat16).astype(jnp.float32)
            decays = [spread(decay_ref, n, cols) for n in range(modes)]
            steps = [jnp.exp(-d) for d in decays]
            states = None
            for j in range(span):
                sig = rows_ref[pl.ds(j, sublanes, stride=span), :]
                sig_ref[pl.ds(j * sublanes, sublanes), cols] = sig
                states = [s * a + sig for s, a in zip(states, steps)] if j else [sig] * modes
            for n in range(modes):
                chunk_ref[n, :, cols] = states[n]
                weighted = states[n] * jnp.exp(-decays[n] * left)
                total_ref[pl.ds(n, 1), cols] = jnp.sum(weighted, axis=0, keepdims=True)
            sent_ref[:, cols] = total_ref[:, cols].astype(jnp.bfloat16)

    for copy in side:
        copy.wait()


def local_kernel(span, piece, decay_ref, res_ref, skip_ref, sig_ref, chunk_ref, v_ref, x_ref, base_ref, conv_ref):
    modes = decay_ref.shape[0]
    run = lax.broadcasted_iota(jnp.int32, (sublanes, lanes), 0)

    def shifted(state, by):
        return jnp.where(run >= by, pltpu.roll(state, by, 0), 0.0)

    @pl.loop(0, piece_width // lanes)
    def _(group):
        cols = at_group(group + piece * (piece_width // lanes))
        skip = jnp.broadcast_to(skip_ref[:, cols], (sublanes, lanes))
        half = modes // 2
        for low in range(0, modes, half):
            steps, gains, states = [], [], []
            for n in range(low, low + half):
                decay = spread(decay_ref, n, cols)
                gain = spread(res_ref, n, cols)
                state = chunk_ref[n, :, cols]
                over = jnp.exp(decay * float(-span))
                for by in (1, 2, 4):
                    state = state + over * shifted(state, by)
                    over = over * over
                states.append(gain * shifted(state, 1))
                steps.append(jnp.exp(-decay))
                gains.append(gain)
            for j in range(span):
                sig = sig_ref[pl.ds(j * sublanes, sublanes), cols]
                states = [s * a + sig * g for s, a, g in zip(states, steps, gains)]
                out = conv_ref.at[pl.ds(j, sublanes, stride=span), :]
                if low == 0:
                    out[...] = tree_sum(states) + skip * sig
                else:
                    out[...] = out[...] + tree_sum(states)
        mixed = v_ref[:, cols].astype(jnp.float32) * conv_ref[...]
        base_ref[:, at_group(group)] = x_ref[:, cols].astype(jnp.float32) + mixed


def merge_kernel(size, rows, last, arrived_ref, decay_ref, *rest):
    if size == 1:
        total_ref, rest = rest[0], rest[1:]
    elif last:
        enter_ref, rest = rest[0], rest[1:]
    else:
        total_ref, enter_ref, rest = rest[0], rest[1], rest[2:]
    position = lax.axis_index("ctx")
    arrived = arrived_ref[...].astype(jnp.float32)
    decay = decay_ref[...]
    upper = (position & size) != 0
    within = (position & (size - 1)).astype(jnp.float32) * float(rows)
    share = jnp.where(upper, arrived, 0.0) * jnp.exp(decay * -within)
    rest[0][...] = share if size == 1 else enter_ref[...] + share
    if not last:
        over = jnp.exp(decay * float(-rows * size))
        total = total_ref[...]
        total = jnp.where(upper, total + over * arrived, over * total + arrived)
        rest[1][...] = total
        rest[2][...] = total.astype(jnp.bfloat16)


def finish_kernel(enter_ref, decay_ref, res_ref, v_ref, *rest):
    base_refs = rest[:-3]
    new_ref, power_ref, acc_ref = rest[-3:]
    modes = decay_ref.shape[0]
    rows = v_ref.shape[0]
    run = lax.broadcasted_iota(jnp.int32, (sublanes, lanes), 0)
    ahead = (run + 1).astype(jnp.float32)
    acc_ref[...] = jnp.zeros_like(acc_ref)
    for piece, base_ref in enumerate(base_refs):

        @pl.loop(0, piece_width // lanes)
        def _(group):
            here = at_group(group)
            cols = at_group(group + piece * (piece_width // lanes))
            steps, states = [], []
            for n in range(modes):
                decay = spread(decay_ref, n, cols)
                start = spread(res_ref, n, cols) * spread(enter_ref, n, cols)
                states.append(start * jnp.exp(-decay * ahead))
                steps.append(jnp.exp(decay * float(-sublanes)))
            for pair in range(rows // (2 * sublanes)):
                halves = []
                for half in range(2):
                    halves.append(tree_sum(states))
                    states = [s * a for s, a in zip(states, steps)]
                at = pl.ds(pair * 2 * sublanes, 2 * sublanes)
                carried = jnp.concatenate(halves, axis=0)
                fresh = base_ref[at, here] + v_ref[at, cols].astype(jnp.float32) * carried
                fresh = fresh.astype(jnp.bfloat16)
                new_ref[at, cols] = fresh
                fresh = fresh.astype(jnp.float32)
                acc_ref[at, :] += fresh * fresh

    ones = jnp.ones((sublanes, lanes), jnp.float32)
    sums = lax.dot_general(
        ones,
        acc_ref[...],
        (((1,), (1,)), ((), ())),
        precision=lax.Precision.HIGHEST,
        preferred_element_type=jnp.float32,
    )
    power_ref[...] = sums[0:1]


def norm_kernel(channels, mine_ref, other_ref, gain_ref, new_ref, out_hbm, inv_ref, out_ref, sem):
    rows, width = new_ref.shape
    power = (mine_ref[...] + other_ref[...]) * (1.0 / channels)
    inverse = lax.rsqrt(power + epsilon)
    inv_ref[...] = jnp.transpose(jnp.broadcast_to(inverse, (lanes, rows)))
    copies = []
    for p in range(width // piece_width):

        @pl.loop(p * piece_width // lanes, (p + 1) * piece_width // lanes)
        def _(group):
            cols = at_group(group)
            scaled = new_ref[:, cols].astype(jnp.float32) * inv_ref[...] * gain_ref[:, cols]
            out_ref[:, cols] = scaled.astype(jnp.bfloat16)

        cols = pl.ds(p * piece_width, piece_width)
        copies.append(pltpu.make_async_copy(out_ref.at[:, cols], out_hbm.at[:, cols], sem.at[p]))
        copies[-1].start()
    for copy in copies:
        copy.wait()


def shards(queries, key_proj, values, residues, decay_rates, skip_weight, stream, norm_gain):
    rows, width = queries.shape
    modes = decay_rates.shape[0]
    span = rows // sublanes
    params = pltpu.CompilerParams(vmem_limit_bytes=vmem_bytes)
    f32, bf16 = jnp.float32, jnp.bfloat16
    in_vmem = pl.BlockSpec(memory_space=pltpu.VMEM)
    anywhere = pl.BlockSpec(memory_space=pl.ANY)
    pieces = width // piece_width

    far = [queries, key_proj, values, stream, decay_rates, residues, skip_weight[None, :]]
    far = [pltpu.with_memory_space_constraint(a, pltpu.HBM) for a in far]
    outs = [
        ((modes, width), f32),
        ((modes, width), bf16),
        ((modes, sublanes, width), f32),
        ((rows, width), f32),
        ((rows, width), bf16),
        ((rows, width), bf16),
        ((modes, width), f32),
        ((modes, width), f32),
        ((1, width), f32),
    ]
    total, sent, chunks, signal, near_values, near_stream, decay, gains, skip = pl.pallas_call(
        functools.partial(state_kernel, span),
        in_specs=[anywhere] * len(far),
        out_specs=[in_vmem] * len(outs),
        out_shape=[pltpu.VMEM(shape, dtype) for shape, dtype in outs],
        scratch_shapes=[
            pltpu.VMEM((rows, width), bf16),
            pltpu.VMEM((rows, width), bf16),
            pltpu.VMEM((rows, lanes), f32),
            pltpu.SemaphoreType.DMA((2, pieces)),
            pltpu.SemaphoreType.DMA((5,)),
        ],
        compiler_params=params,
        cost_estimate=pl.CostEstimate(flops=2 * modes * rows * width, bytes_accessed=4 * rows * width, transcendentals=0),
        name="states",
    )(*far)

    def local_piece(piece, decay):
        return pl.pallas_call(
            functools.partial(local_kernel, span, piece),
            in_specs=[in_vmem] * 7,
            out_specs=in_vmem,
            out_shape=pltpu.VMEM((rows, piece_width), f32),
            scratch_shapes=[pltpu.VMEM((rows, lanes), f32)],
            compiler_params=params,
            cost_estimate=pl.CostEstimate(
                flops=4 * modes * rows * piece_width, bytes_accessed=12 * rows * piece_width, transcendentals=0
            ),
            name="local",
        )(decay, gains, skip, signal, chunks, near_values, near_stream)

    def link(partner_of):
        places = [(z, y, x) for z in range(8) for y in range(2) for x in range(4)]
        index = lambda z, y, x: (z * 2 + y) * 4 + x
        return [(index(*at), index(*partner_of(*at))) for at in places]

    rounds = [
        link(lambda z, y, x: (z, y, x ^ 1)),
        link(lambda z, y, x: (z, y, x ^ 3)),
        link(lambda z, y, x: (z, y ^ 1, x)),
        link(lambda z, y, x: (z ^ 1, y, x)),
        link(lambda z, y, x: (z ^ 2, y, x)),
        link(lambda z, y, x: (7 - z, y, x)),
    ]
    def merge(size, last, arrived, total, enter):
        operands = [arrived, decay] + ([] if last else [total]) + ([] if size == 1 else [enter])
        outs = [f32] if last else [f32, f32, bf16]
        return pl.pallas_call(
            functools.partial(merge_kernel, size, rows, last),
            in_specs=[in_vmem] * len(operands),
            out_specs=[in_vmem] * len(outs),
            out_shape=[pltpu.VMEM((modes, width), dtype) for dtype in outs],
            compiler_params=params,
            name="merge",
        )(*operands)

    enter = None
    bases = []
    for level, pairs in enumerate(rounds):
        arrived = lax.ppermute(sent, "ctx", pairs)
        if level < pieces:
            tied, sent = lax.optimization_barrier((decay, sent))
            base = local_piece(level, tied)
            arrived, base = lax.optimization_barrier((arrived, base))
            bases.append(base)
        if level + 1 < len(rounds):
            enter, total, sent = merge(1 << level, False, arrived, total, enter)
        else:
            (enter,) = merge(1 << level, True, arrived, None, enter)

    fresh, power = pl.pallas_call(
        finish_kernel,
        in_specs=[in_vmem] * (4 + pieces),
        out_specs=[in_vmem] * 2,
        out_shape=[pltpu.VMEM((rows, width), bf16), pltpu.VMEM((1, rows), f32)],
        scratch_shapes=[pltpu.VMEM((rows, lanes), f32)],
        compiler_params=params,
        cost_estimate=pl.CostEstimate(flops=2 * modes * rows * width, bytes_accessed=8 * rows * width, transcendentals=0),
        name="finish",
    )(enter, decay, gains, near_values, *bases)

    power = power + lax.ppermute(power, "tp", [(i, i ^ 1) for i in range(4)])
    other = lax.ppermute(power, "tp", [(i, i ^ 3) for i in range(4)])

    channels = width * lax.axis_size("tp")
    normed = pl.pallas_call(
        functools.partial(norm_kernel, channels),
        in_specs=[in_vmem] * 4,
        out_specs=anywhere,
        out_shape=pltpu.HBM((rows, width), bf16),
        scratch_shapes=[
            pltpu.VMEM((rows, lanes), f32),
            pltpu.VMEM((rows, width), bf16),
            pltpu.SemaphoreType.DMA((pieces,)),
        ],
        compiler_params=params,
        name="normalise",
    )(power, other, norm_gain[None, :], fresh)
    return (fresh, normed)


def solution(mesh):
    in_specs = (
        P("ctx", "tp"),
        P("ctx", "tp"),
        P("ctx", "tp"),
        P(None, "tp"),
        P(None, "tp"),
        P("tp"),
        P("ctx", "tp"),
        P("tp"),
    )
    out_specs = (P("ctx", "tp"), P("ctx", "tp"))
    return jax.shard_map(shards, mesh=mesh, in_specs=in_specs, out_specs=out_specs, check_vma=False)
```

```python
import functools

import jax
import jax.numpy as jnp
from jax import lax
from jax.experimental import pallas as pl
from jax.experimental.pallas import tpu as pltpu
from jax.sharding import PartitionSpec as P

epsilon = 1e-06
lanes = 128
sublanes = 8
piece_width = 512
vmem_bytes = 24 * 1024 * 1024


def at_group(group):
    return pl.ds(pl.multiple_of(group * lanes, lanes), lanes)


def spread(ref, mode, cols):
    return jnp.broadcast_to(ref[pl.ds(mode, 1), cols], (sublanes, lanes))


def tree_sum(parts):
    parts = list(parts)
    while len(parts) > 1:
        parts = [l + r for l, r in zip(parts[::2], parts[1::2])]
    return parts[0]


def state_kernel(
    q_hbm, k_hbm, v_hbm, x_hbm, decay_hbm, res_hbm, skip_hbm,
    total_ref, sent_ref, sig_ref, v_ref, x_ref, decay_ref, res_ref, skip_ref, tile_ref,
    q_ref, k_ref, over_ref, pair_sem, side_sem,
):
    modes = decay_ref.shape[0]
    rows, width = q_ref.shape
    edges = [0, 256, 512] + list(range(1024, width + 1, 512))
    pair = []
    first = pltpu.make_async_copy(decay_hbm, decay_ref, side_sem.at[0])
    first.start()
    for p, (low, high) in enumerate(zip(edges, edges[1:])):
        cols = pl.ds(low, high - low)
        for at, (src, dst) in enumerate(((q_hbm, q_ref), (k_hbm, k_ref))):
            pair.append(pltpu.make_async_copy(src.at[:, cols], dst.at[:, cols], pair_sem.at[at, p]))
            pair[-1].start()
    side = []
    for at, (src, dst) in enumerate(((res_hbm, res_ref), (skip_hbm, skip_ref), (v_hbm, v_ref), (x_hbm, x_ref))):
        side.append(pltpu.make_async_copy(src, dst, side_sem.at[at + 1]))
        side[-1].start()
    first.wait()
    decay = decay_ref[...]
    tile_ref[...] = jnp.exp(decay * float(-sublanes))
    for at in range(3):
        over_ref[pl.ds(at * modes, modes), :] = jnp.exp(decay * float(-1 << at))
    for p, (low, high) in enumerate(zip(edges, edges[1:])):
        pair[2 * p].wait()
        pair[2 * p + 1].wait()

        @pl.loop(low // lanes, high // lanes)
        def _(group):
            cols = at_group(group)
            steps = [spread(tile_ref, n, cols) for n in range(modes)]
            states = None
            for j in range(0, rows, 2 * sublanes):
                at = pl.ds(j, 2 * sublanes)
                sig = q_ref[at, cols] * k_ref[at, cols]
                sig_ref[at, cols] = sig
                sig = sig.astype(jnp.float32)
                for part in (sig[:sublanes], sig[sublanes:]):
                    states = [s * a + part for s, a in zip(states, steps)] if states else [part] * modes
            for n in range(modes):
                state = states[n]
                for at in range(3):
                    state = state + spread(over_ref, at * modes + n, cols) * pltpu.roll(state, 1 << at, 0)
                total_ref[pl.ds(n, 1), cols] = state[sublanes - 1 :]
            sent_ref[:, cols] = total_ref[:, cols].astype(jnp.bfloat16)

    for copy in side:
        copy.wait()


def local_kernel(
    piece, decay_ref, res_ref, skip_ref, sig_ref, v_ref, x_ref, base_ref, lead_ref, rows_ref, runs_ref, conv_ref
):
    modes = decay_ref.shape[0]
    span = sig_ref.shape[0] // sublanes
    run = lax.broadcasted_iota(jnp.int32, (sublanes, lanes), 0)
    ahead = (run + 1).astype(jnp.float32)

    def shifted(state, by):
        return jnp.where(run >= by, pltpu.roll(state, by, 0), 0.0)

    @pl.loop(0, piece_width // lanes)
    def _(group):
        here = at_group(group)
        cols = at_group(group + piece * (piece_width // lanes))
        rows_ref[...] = sig_ref[:, cols].astype(jnp.float32)
        for j in range(span):
            runs_ref[pl.ds(j * sublanes, sublanes), :] = rows_ref[pl.ds(j, sublanes, stride=span), :]
        skip = jnp.broadcast_to(skip_ref[:, cols], (sublanes, lanes))
        half = modes // 2
        for low in range(0, modes, half):
            decays = [spread(decay_ref, n, cols) for n in range(low, low + half)]
            gains = [spread(res_ref, n, cols) for n in range(low, low + half)]
            steps = [jnp.exp(-d) for d in decays]
            states = None
            for j in range(span):
                sig = runs_ref[pl.ds(j * sublanes, sublanes), :]
                states = [s * a + sig for s, a in zip(states, steps)] if j else [sig] * half
            for n in range(half):
                state = states[n]
                over = jnp.exp(decays[n] * float(-span))
                for by in (1, 2, 4):
                    state = state + over * shifted(state, by)
                    over = over * over
                states[n] = gains[n] * shifted(state, 1)
                lead_ref[low + n, :, here] = gains[n] * jnp.exp(-decays[n] * ahead)
            for j in range(span):
                sig = runs_ref[pl.ds(j * sublanes, sublanes), :]
                states = [s * a + sig * g for s, a, g in zip(states, steps, gains)]
                out = conv_ref.at[pl.ds(j, sublanes, stride=span), :]
                if low == 0:
                    out[...] = tree_sum(states) + skip * sig
                else:
                    out[...] = out[...] + tree_sum(states)
        mixed = v_ref[:, cols].astype(jnp.float32) * conv_ref[...]
        base_ref[:, here] = x_ref[:, cols].astype(jnp.float32) + mixed


def merge_kernel(size, rows, last, arrived_ref, decay_ref, *rest):
    if size == 1:
        total_ref, rest = rest[0], rest[1:]
    elif last:
        enter_ref, rest = rest[0], rest[1:]
    else:
        total_ref, enter_ref, rest = rest[0], rest[1], rest[2:]
    position = lax.axis_index("ctx")
    arrived = arrived_ref[...].astype(jnp.float32)
    decay = decay_ref[...]
    upper = (position & size) != 0
    within = (position & (size - 1)).astype(jnp.float32) * float(rows)
    share = jnp.where(upper, arrived, 0.0) * jnp.exp(decay * -within)
    rest[0][...] = share if size == 1 else enter_ref[...] + share
    if not last:
        over = jnp.exp(decay * float(-rows * size))
        total = total_ref[...]
        total = jnp.where(upper, total + over * arrived, over * total + arrived)
        rest[1][...] = total.astype(jnp.bfloat16)
        if len(rest) > 2:
            rest[2][...] = total


def finish_kernel(enter_ref, tile_ref, v_ref, *rest):
    pieces = (len(rest) - 3) // 2
    base_refs, lead_refs = rest[:pieces], rest[pieces:-3]
    new_ref, power_ref, acc_ref = rest[-3:]
    modes = tile_ref.shape[0]
    rows = v_ref.shape[0]
    acc_ref[...] = jnp.zeros_like(acc_ref)
    for piece, (base_ref, lead_ref) in enumerate(zip(base_refs, lead_refs)):

        @pl.loop(0, piece_width // lanes)
        def _(group):
            here = at_group(group)
            cols = at_group(group + piece * (piece_width // lanes))
            steps = [spread(tile_ref, n, cols) for n in range(modes)]
            states = [lead_ref[n, :, here] * spread(enter_ref, n, cols) for n in range(modes)]
            for pair in range(rows // (2 * sublanes)):
                halves = []
                for half in range(2):
                    halves.append(tree_sum(states))
                    states = [s * a for s, a in zip(states, steps)]
                at = pl.ds(pair * 2 * sublanes, 2 * sublanes)
                carried = jnp.concatenate(halves, axis=0)
                fresh = base_ref[at, here] + v_ref[at, cols].astype(jnp.float32) * carried
                fresh = fresh.astype(jnp.bfloat16)
                new_ref[at, cols] = fresh
                fresh = fresh.astype(jnp.float32)
                acc_ref[at, :] += fresh * fresh

    ones = jnp.ones((sublanes, lanes), jnp.float32)
    sums = lax.dot_general(
        ones,
        acc_ref[...],
        (((1,), (1,)), ((), ())),
        precision=lax.Precision.HIGHEST,
        preferred_element_type=jnp.float32,
    )
    power_ref[...] = sums[0:1]


def norm_kernel(channels, mine_ref, other_ref, gain_ref, new_ref, out_hbm, inv_ref, out_ref, sem):
    rows, width = new_ref.shape
    power = (mine_ref[...] + other_ref[...]) * (1.0 / channels)
    inverse = lax.rsqrt(power + epsilon)
    inv_ref[...] = jnp.transpose(jnp.broadcast_to(inverse, (lanes, rows)))
    copies = []
    part = width // sem.shape[0]
    for p in range(sem.shape[0]):

        @pl.loop(p * part // lanes, (p + 1) * part // lanes)
        def _(group):
            cols = at_group(group)
            scaled = new_ref[:, cols].astype(jnp.float32) * inv_ref[...] * gain_ref[:, cols]
            out_ref[:, cols] = scaled.astype(jnp.bfloat16)

        cols = pl.ds(p * part, part)
        copies.append(pltpu.make_async_copy(out_ref.at[:, cols], out_hbm.at[:, cols], sem.at[p]))
        copies[-1].start()
    for copy in copies:
        copy.wait()


def shards(queries, key_proj, values, residues, decay_rates, skip_weight, stream, norm_gain):
    rows, width = queries.shape
    modes = decay_rates.shape[0]
    params = pltpu.CompilerParams(vmem_limit_bytes=vmem_bytes)
    f32, bf16 = jnp.float32, jnp.bfloat16
    in_vmem = pl.BlockSpec(memory_space=pltpu.VMEM)
    anywhere = pl.BlockSpec(memory_space=pl.ANY)
    pieces = width // piece_width

    far = [queries, key_proj, values, stream, decay_rates, residues, skip_weight[None, :]]
    far = [pltpu.with_memory_space_constraint(a, pltpu.HBM) for a in far]
    outs = [
        ((modes, width), f32),
        ((modes, width), bf16),
        ((rows, width), bf16),
        ((rows, width), bf16),
        ((rows, width), bf16),
        ((modes, width), f32),
        ((modes, width), f32),
        ((1, width), f32),
        ((modes, width), f32),
    ]
    total, sent, signal, near_values, near_stream, decay, gains, skip, tile = pl.pallas_call(
        state_kernel,
        in_specs=[anywhere] * len(far),
        out_specs=[in_vmem] * len(outs),
        out_shape=[pltpu.VMEM(shape, dtype) for shape, dtype in outs],
        scratch_shapes=[
            pltpu.VMEM((rows, width), bf16),
            pltpu.VMEM((rows, width), bf16),
            pltpu.VMEM((3 * modes, width), f32),
            pltpu.SemaphoreType.DMA((2, pieces + 1)),
            pltpu.SemaphoreType.DMA((5,)),
        ],
        compiler_params=params,
        cost_estimate=pl.CostEstimate(flops=2 * modes * rows * width, bytes_accessed=4 * rows * width, transcendentals=0),
        name="states",
    )(*far)

    def local_piece(piece, decay):
        return pl.pallas_call(
            functools.partial(local_kernel, piece),
            in_specs=[in_vmem] * 6,
            out_specs=[in_vmem] * 2,
            out_shape=[pltpu.VMEM((rows, piece_width), f32), pltpu.VMEM((modes, sublanes, piece_width), f32)],
            scratch_shapes=[pltpu.VMEM((rows, lanes), f32)] * 3,
            compiler_params=params,
            cost_estimate=pl.CostEstimate(
                flops=6 * modes * rows * piece_width, bytes_accessed=12 * rows * piece_width, transcendentals=0
            ),
            name="local",
        )(decay, gains, skip, signal, near_values, near_stream)

    def link(partner_of):
        places = [(z, y, x) for z in range(8) for y in range(2) for x in range(4)]
        index = lambda z, y, x: (z * 2 + y) * 4 + x
        return [(index(*at), index(*partner_of(*at))) for at in places]

    rounds = [
        link(lambda z, y, x: (z, y, x ^ 1)),
        link(lambda z, y, x: (z, y, x ^ 3)),
        link(lambda z, y, x: (z, y ^ 1, x)),
        link(lambda z, y, x: (z ^ 1, y, x)),
        link(lambda z, y, x: (z ^ 2, y, x)),
        link(lambda z, y, x: ((6, 7, 4, 5, 2, 3, 0, 1)[z], y, x)),
    ]
    def merge(size, last, keep, arrived, total, enter):
        operands = [arrived, decay] + ([] if last else [total]) + ([] if size == 1 else [enter])
        outs = [f32] if last else [f32, bf16, f32] if keep else [f32, bf16]
        return pl.pallas_call(
            functools.partial(merge_kernel, size, rows, last),
            in_specs=[in_vmem] * len(operands),
            out_specs=[in_vmem] * len(outs),
            out_shape=[pltpu.VMEM((modes, width), dtype) for dtype in outs],
            compiler_params=params,
            name="merge",
        )(*operands)

    enter = None
    bases, leads = [], []
    for level, pairs in enumerate(rounds):
        arrived = lax.ppermute(sent, "ctx", pairs)
        if level < pieces:
            tied, sent = lax.optimization_barrier((decay, sent))
            base, lead = local_piece(level, tied)
            arrived, base = lax.optimization_barrier((arrived, base))
            bases.append(base)
            leads.append(lead)
        last = level + 1 == len(rounds)
        keep = level + 2 < len(rounds)
        merged = merge(1 << level, last, keep, arrived, total, enter)
        enter = merged[0]
        if not last:
            sent = merged[1]
        if keep:
            total = merged[2]

    fresh, power = pl.pallas_call(
        finish_kernel,
        in_specs=[in_vmem] * (3 + 2 * pieces),
        out_specs=[in_vmem] * 2,
        out_shape=[pltpu.VMEM((rows, width), bf16), pltpu.VMEM((1, rows), f32)],
        scratch_shapes=[pltpu.VMEM((rows, lanes), f32)],
        compiler_params=params,
        cost_estimate=pl.CostEstimate(flops=2 * modes * rows * width, bytes_accessed=8 * rows * width, transcendentals=0),
        name="finish",
    )(enter, tile, near_values, *bases, *leads)

    power = power + lax.ppermute(power, "tp", [(i, i ^ 1) for i in range(4)])
    other = lax.ppermute(power, "tp", [(i, i ^ 3) for i in range(4)])

    channels = width * lax.axis_size("tp")
    normed = pl.pallas_call(
        functools.partial(norm_kernel, channels),
        in_specs=[in_vmem] * 4,
        out_specs=anywhere,
        out_shape=pltpu.HBM((rows, width), bf16),
        scratch_shapes=[
            pltpu.VMEM((rows, lanes), f32),
            pltpu.VMEM((rows, width), bf16),
            pltpu.SemaphoreType.DMA((8,)),
        ],
        compiler_params=params,
        name="normalise",
    )(power, other, norm_gain[None, :], fresh)
    return (fresh, normed)


def solution(mesh):
    in_specs = (
        P("ctx", "tp"),
        P("ctx", "tp"),
        P("ctx", "tp"),
        P(None, "tp"),
        P(None, "tp"),
        P("tp"),
        P("ctx", "tp"),
        P("tp"),
    )
    out_specs = (P("ctx", "tp"), P("ctx", "tp"))
    return jax.shard_map(shards, mesh=mesh, in_specs=in_specs, out_specs=out_specs, check_vma=False)
```

```python
import functools

import jax
import jax.numpy as jnp
from jax import lax
from jax.experimental import pallas as pl
from jax.experimental.pallas import tpu as pltpu
from jax.sharding import PartitionSpec as P

epsilon = 1e-06
lanes = 128
sublanes = 8
piece_width = 256
pieces_beside = (2, 3, 3)
send_order = ((1, 2, 0), (2, 0, 1), (1, 2, 0))
vmem_bytes = 24 * 1024 * 1024


def at_group(group):
    return pl.ds(pl.multiple_of(group * lanes, lanes), lanes)


def spread(ref, mode, cols):
    return jnp.broadcast_to(ref[pl.ds(mode, 1), cols], (sublanes, lanes))


def tree_sum(parts):
    parts = list(parts)
    while len(parts) > 1:
        parts = [l + r for l, r in zip(parts[::2], parts[1::2])]
    return parts[0]


def state_kernel(
    q_hbm, k_hbm, v_hbm, x_hbm, decay_hbm, res_hbm, skip_hbm,
    total_ref, sent_ref, sig_ref, v_ref, x_ref, decay_ref, res_ref, skip_ref, tile_ref,
    q_ref, k_ref, over_ref, pair_sem, side_sem,
):
    modes = decay_ref.shape[0]
    rows, width = q_ref.shape
    edges = [0, 256, 512] + list(range(1024, width + 1, 512))
    pair = []
    first = pltpu.make_async_copy(decay_hbm, decay_ref, side_sem.at[0])
    first.start()
    for p, (low, high) in enumerate(zip(edges, edges[1:])):
        cols = pl.ds(low, high - low)
        for at, (src, dst) in enumerate(((q_hbm, q_ref), (k_hbm, k_ref))):
            pair.append(pltpu.make_async_copy(src.at[:, cols], dst.at[:, cols], pair_sem.at[at, p]))
            pair[-1].start()
    side = []
    for at, (src, dst) in enumerate(((res_hbm, res_ref), (skip_hbm, skip_ref), (v_hbm, v_ref), (x_hbm, x_ref))):
        side.append(pltpu.make_async_copy(src, dst, side_sem.at[at + 1]))
        side[-1].start()
    first.wait()
    decay = decay_ref[...]
    tile_ref[...] = jnp.exp(decay * float(-sublanes))
    for at in range(3):
        over_ref[pl.ds(at * modes, modes), :] = jnp.exp(decay * float(-1 << at))
    for p, (low, high) in enumerate(zip(edges, edges[1:])):
        pair[2 * p].wait()
        pair[2 * p + 1].wait()

        @pl.loop(low // lanes, high // lanes)
        def _(group):
            cols = at_group(group)
            steps = [spread(tile_ref, n, cols) for n in range(modes)]
            states = None
            for j in range(0, rows, 2 * sublanes):
                at = pl.ds(j, 2 * sublanes)
                sig = q_ref[at, cols] * k_ref[at, cols]
                sig_ref[at, cols] = sig
                sig = sig.astype(jnp.float32)
                for part in (sig[:sublanes], sig[sublanes:]):
                    states = [s * a + part for s, a in zip(states, steps)] if states else [part] * modes
            for n in range(modes):
                state = states[n]
                for at in range(3):
                    state = state + spread(over_ref, at * modes + n, cols) * pltpu.roll(state, 1 << at, 0)
                total_ref[pl.ds(n, 1), cols] = state[sublanes - 1 :]
            sent_ref[:, cols] = total_ref[:, cols].astype(jnp.bfloat16)

    for copy in side:
        copy.wait()


def local_kernel(
    piece, decay_ref, res_ref, skip_ref, sig_ref, v_ref, x_ref, base_ref, lead_ref, rows_ref, runs_ref, conv_ref
):
    modes = decay_ref.shape[0]
    span = sig_ref.shape[0] // sublanes
    run = lax.broadcasted_iota(jnp.int32, (sublanes, lanes), 0)
    ahead = (run + 1).astype(jnp.float32)

    def shifted(state, by):
        return jnp.where(run >= by, pltpu.roll(state, by, 0), 0.0)

    @pl.loop(0, piece_width // lanes)
    def _(group):
        here = at_group(group)
        cols = at_group(group + piece * (piece_width // lanes))
        rows_ref[...] = sig_ref[:, cols].astype(jnp.float32)
        for j in range(span):
            runs_ref[pl.ds(j * sublanes, sublanes), :] = rows_ref[pl.ds(j, sublanes, stride=span), :]
        skip = jnp.broadcast_to(skip_ref[:, cols], (sublanes, lanes))
        half = modes // 2
        for low in range(0, modes, half):
            decays = [spread(decay_ref, n, cols) for n in range(low, low + half)]
            gains = [spread(res_ref, n, cols) for n in range(low, low + half)]
            steps = [jnp.exp(-d) for d in decays]
            states = None
            for j in range(span):
                sig = runs_ref[pl.ds(j * sublanes, sublanes), :]
                states = [s * a + sig for s, a in zip(states, steps)] if j else [sig] * half
            for n in range(half):
                state = states[n]
                over = jnp.exp(decays[n] * float(-span))
                for by in (1, 2, 4):
                    state = state + over * shifted(state, by)
                    over = over * over
                states[n] = gains[n] * shifted(state, 1)
                lead_ref[low + n, :, here] = gains[n] * jnp.exp(-decays[n] * ahead)
            for j in range(span):
                sig = runs_ref[pl.ds(j * sublanes, sublanes), :]
                states = [s * a + sig * g for s, a, g in zip(states, steps, gains)]
                out = conv_ref.at[pl.ds(j, sublanes, stride=span), :]
                if low == 0:
                    out[...] = tree_sum(states) + skip * sig
                else:
                    out[...] = out[...] + tree_sum(states)
        mixed = v_ref[:, cols].astype(jnp.float32) * conv_ref[...]
        base_ref[:, here] = x_ref[:, cols].astype(jnp.float32) + mixed


def merge_kernel(size, rows, order, first, last, decay_ref, total_ref, *rest):
    position = lax.axis_index("ctx")
    odd = (position & size) != 0
    high = (position & (2 * size)) != 0
    decay = decay_ref[...]
    near, far, across = (rest[order.index(at)][...].astype(jnp.float32) for at in range(3))
    rest = rest[3:]
    over = jnp.exp(decay * float(-rows * size))
    other = jnp.where(odd, across * over + far, far * over + across)
    enter = jnp.where(high, jnp.where(odd, other * over, other), 0.0) + jnp.where(odd, near, 0.0)
    if not first:
        within = (position & (size - 1)).astype(jnp.float32) * float(rows)
        enter = rest[0][...] + enter * jnp.exp(decay * -within)
        rest = rest[1:]
    rest[0][...] = enter
    if not last:
        total = total_ref[...]
        own = jnp.where(odd, near * over + total, total * over + near)
        whole = jnp.where(high, other * (over * over) + own, own * (over * over) + other)
        rest[1][...] = whole.astype(jnp.bfloat16)
        rest[2][...] = whole


def finish_kernel(enter_ref, tile_ref, v_ref, *rest):
    pieces = (len(rest) - 3) // 2
    base_refs, lead_refs = rest[:pieces], rest[pieces:-3]
    new_ref, power_ref, acc_ref = rest[-3:]
    modes = tile_ref.shape[0]
    rows = v_ref.shape[0]
    acc_ref[...] = jnp.zeros_like(acc_ref)
    for piece, (base_ref, lead_ref) in enumerate(zip(base_refs, lead_refs)):

        @pl.loop(0, piece_width // lanes)
        def _(group):
            here = at_group(group)
            cols = at_group(group + piece * (piece_width // lanes))
            steps = [spread(tile_ref, n, cols) for n in range(modes)]
            states = [lead_ref[n, :, here] * spread(enter_ref, n, cols) for n in range(modes)]
            for pair in range(rows // (2 * sublanes)):
                halves = []
                for half in range(2):
                    halves.append(tree_sum(states))
                    states = [s * a for s, a in zip(states, steps)]
                at = pl.ds(pair * 2 * sublanes, 2 * sublanes)
                carried = jnp.concatenate(halves, axis=0)
                fresh = base_ref[at, here] + v_ref[at, cols].astype(jnp.float32) * carried
                fresh = fresh.astype(jnp.bfloat16)
                new_ref[at, cols] = fresh
                fresh = fresh.astype(jnp.float32)
                acc_ref[at, :] += fresh * fresh

    ones = jnp.ones((sublanes, lanes), jnp.float32)
    sums = lax.dot_general(
        ones,
        acc_ref[...],
        (((1,), (1,)), ((), ())),
        precision=lax.Precision.HIGHEST,
        preferred_element_type=jnp.float32,
    )
    power_ref[...] = sums[0:1]


def norm_kernel(channels, mine_ref, other_ref, gain_ref, new_ref, out_hbm, inv_ref, out_ref, sem):
    rows, width = new_ref.shape
    power = (mine_ref[...] + other_ref[...]) * (1.0 / channels)
    inverse = lax.rsqrt(power + epsilon)
    inv_ref[...] = jnp.transpose(jnp.broadcast_to(inverse, (lanes, rows)))
    copies = []
    part = width // sem.shape[0]
    for p in range(sem.shape[0]):

        @pl.loop(p * part // lanes, (p + 1) * part // lanes)
        def _(group):
            cols = at_group(group)
            scaled = new_ref[:, cols].astype(jnp.float32) * inv_ref[...] * gain_ref[:, cols]
            out_ref[:, cols] = scaled.astype(jnp.bfloat16)

        cols = pl.ds(p * part, part)
        copies.append(pltpu.make_async_copy(out_ref.at[:, cols], out_hbm.at[:, cols], sem.at[p]))
        copies[-1].start()
    for copy in copies:
        copy.wait()


def shards(queries, key_proj, values, residues, decay_rates, skip_weight, stream, norm_gain):
    rows, width = queries.shape
    modes = decay_rates.shape[0]
    params = pltpu.CompilerParams(vmem_limit_bytes=vmem_bytes)
    f32, bf16 = jnp.float32, jnp.bfloat16
    in_vmem = pl.BlockSpec(memory_space=pltpu.VMEM)
    anywhere = pl.BlockSpec(memory_space=pl.ANY)
    pieces = width // piece_width

    far = [queries, key_proj, values, stream, decay_rates, residues, skip_weight[None, :]]
    far = [pltpu.with_memory_space_constraint(a, pltpu.HBM) for a in far]
    outs = [
        ((modes, width), f32),
        ((modes, width), bf16),
        ((rows, width), bf16),
        ((rows, width), bf16),
        ((rows, width), bf16),
        ((modes, width), f32),
        ((modes, width), f32),
        ((1, width), f32),
        ((modes, width), f32),
    ]
    total, sent, signal, near_values, near_stream, decay, gains, skip, tile = pl.pallas_call(
        state_kernel,
        in_specs=[anywhere] * len(far),
        out_specs=[in_vmem] * len(outs),
        out_shape=[pltpu.VMEM(shape, dtype) for shape, dtype in outs],
        scratch_shapes=[
            pltpu.VMEM((rows, width), bf16),
            pltpu.VMEM((rows, width), bf16),
            pltpu.VMEM((3 * modes, width), f32),
            pltpu.SemaphoreType.DMA((2, pieces + 1)),
            pltpu.SemaphoreType.DMA((5,)),
        ],
        compiler_params=params,
        cost_estimate=pl.CostEstimate(flops=2 * modes * rows * width, bytes_accessed=4 * rows * width, transcendentals=0),
        name="states",
    )(*far)

    def local_piece(piece, decay):
        return pl.pallas_call(
            functools.partial(local_kernel, piece),
            in_specs=[in_vmem] * 6,
            out_specs=[in_vmem] * 2,
            out_shape=[pltpu.VMEM((rows, piece_width), f32), pltpu.VMEM((modes, sublanes, piece_width), f32)],
            scratch_shapes=[pltpu.VMEM((rows, lanes), f32)] * 3,
            compiler_params=params,
            cost_estimate=pl.CostEstimate(
                flops=6 * modes * rows * piece_width, bytes_accessed=12 * rows * piece_width, transcendentals=0
            ),
            name="local",
        )(decay, gains, skip, signal, near_values, near_stream)

    def link(partner_of):
        places = [(z, y, x) for z in range(8) for y in range(2) for x in range(4)]
        index = lambda z, y, x: (z * 2 + y) * 4 + x
        return [(index(*at), index(*partner_of(*at))) for at in places]

    stages = [
        [link(lambda z, y, x, k=k: (z, y, x ^ k)) for k in (1, 2, 3)],
        [link(lambda z, y, x, k=k: (z ^ (k >> 1), y ^ (k & 1), x)) for k in (1, 2, 3)],
        [link(lambda z, y, x, k=k: (z ^ k, y, x)) for k in (2, 5, 6)],
    ]

    def merge(size, order, last, total, arrived, enter):
        operands = [decay, total, *arrived] + ([] if enter is None else [enter])
        outs = [f32] if last else [f32, bf16, f32]
        return pl.pallas_call(
            functools.partial(merge_kernel, size, rows, order, enter is None, last),
            in_specs=[in_vmem] * len(operands),
            out_specs=[in_vmem] * len(outs),
            out_shape=[pltpu.VMEM((modes, width), dtype) for dtype in outs],
            compiler_params=params,
            name="merge",
        )(*operands)

    enter = None
    bases, leads = [], []
    for level, (links, beside) in enumerate(zip(stages, pieces_beside)):
        order = send_order[level]
        arrived = [lax.ppermute(sent, "ctx", links[at]) for at in order]
        tied, sent = lax.optimization_barrier((decay, sent))
        made = [local_piece(len(bases) + at, tied) for at in range(beside)]
        arrived, made = lax.optimization_barrier((arrived, made))
        bases += [base for base, _ in made]
        leads += [lead for _, lead in made]
        last = level + 1 == len(stages)
        merged = merge(4**level, order, last, total, arrived, enter)
        enter = merged[0]
        if not last:
            sent, total = merged[1:]

    fresh, power = pl.pallas_call(
        finish_kernel,
        in_specs=[in_vmem] * (3 + 2 * pieces),
        out_specs=[in_vmem] * 2,
        out_shape=[pltpu.VMEM((rows, width), bf16), pltpu.VMEM((1, rows), f32)],
        scratch_shapes=[pltpu.VMEM((rows, lanes), f32)],
        compiler_params=params,
        cost_estimate=pl.CostEstimate(flops=2 * modes * rows * width, bytes_accessed=8 * rows * width, transcendentals=0),
        name="finish",
    )(enter, tile, near_values, *bases, *leads)

    power = power + lax.ppermute(power, "tp", [(i, i ^ 1) for i in range(4)])
    other = lax.ppermute(power, "tp", [(i, i ^ 3) for i in range(4)])

    channels = width * lax.axis_size("tp")
    normed = pl.pallas_call(
        functools.partial(norm_kernel, channels),
        in_specs=[in_vmem] * 4,
        out_specs=anywhere,
        out_shape=pltpu.HBM((rows, width), bf16),
        scratch_shapes=[
            pltpu.VMEM((rows, lanes), f32),
            pltpu.VMEM((rows, width), bf16),
            pltpu.SemaphoreType.DMA((8,)),
        ],
        compiler_params=params,
        name="normalise",
    )(power, other, norm_gain[None, :], fresh)
    return (fresh, normed)


def solution(mesh):
    in_specs = (
        P("ctx", "tp"),
        P("ctx", "tp"),
        P("ctx", "tp"),
        P(None, "tp"),
        P(None, "tp"),
        P("tp"),
        P("ctx", "tp"),
        P("tp"),
    )
    out_specs = (P("ctx", "tp"), P("ctx", "tp"))
    return jax.shard_map(shards, mesh=mesh, in_specs=in_specs, out_specs=out_specs, check_vma=False)
```

```python
import functools

import jax
import jax.numpy as jnp
from jax import lax
from jax.experimental import pallas as pl
from jax.experimental.pallas import tpu as pltpu
from jax.sharding import PartitionSpec as P

epsilon = 1e-06
lanes = 128
sublanes = 8
piece_width = 256
pieces_beside = (2, 3, 3)
send_order = ((1, 2, 0), (2, 0, 1), (1, 2, 0))
vmem_bytes = 24 * 1024 * 1024


def at_group(group):
    return pl.ds(pl.multiple_of(group * lanes, lanes), lanes)


def spread(ref, mode, cols):
    return jnp.broadcast_to(ref[pl.ds(mode, 1), cols], (sublanes, lanes))


def tree_sum(parts):
    parts = list(parts)
    while len(parts) > 1:
        parts = [l + r for l, r in zip(parts[::2], parts[1::2])]
    return parts[0]


def state_kernel(
    q_hbm, k_hbm, v_hbm, x_hbm, decay_hbm, res_hbm, skip_hbm,
    total_ref, sent_ref, sig_ref, v_ref, x_ref, decay_ref, res_ref, skip_ref, tile_ref,
    q_ref, k_ref, over_ref, pair_sem, side_sem,
):
    modes = decay_ref.shape[0]
    rows, width = q_ref.shape
    edges = [0, 256, 1024, width]
    pair = []
    first = pltpu.make_async_copy(decay_hbm, decay_ref, side_sem.at[0])
    first.start()
    for p, (low, high) in enumerate(zip(edges, edges[1:])):
        cols = pl.ds(low, high - low)
        for at, (src, dst) in enumerate(((q_hbm, q_ref), (k_hbm, k_ref))):
            pair.append(pltpu.make_async_copy(src.at[:, cols], dst.at[:, cols], pair_sem.at[at, p]))
            pair[-1].start()
    side = []
    for at, (src, dst) in enumerate(((res_hbm, res_ref), (skip_hbm, skip_ref), (v_hbm, v_ref), (x_hbm, x_ref))):
        side.append(pltpu.make_async_copy(src, dst, side_sem.at[at + 1]))
        side[-1].start()
    first.wait()
    decay = decay_ref[...]
    tile_ref[...] = jnp.exp(decay * float(-sublanes))
    for at in range(3):
        over_ref[pl.ds(at * modes, modes), :] = jnp.exp(decay * float(-1 << at))
    for p, (low, high) in enumerate(zip(edges, edges[1:])):
        pair[2 * p].wait()
        pair[2 * p + 1].wait()

        @pl.loop(low // lanes, high // lanes, unroll=2)
        def _(group):
            cols = at_group(group)
            steps = [spread(tile_ref, n, cols) for n in range(modes)]
            states = None
            for j in range(0, rows, 2 * sublanes):
                at = pl.ds(j, 2 * sublanes)
                sig = q_ref[at, cols] * k_ref[at, cols]
                sig_ref[at, cols] = sig
                sig = sig.astype(jnp.float32)
                for part in (sig[:sublanes], sig[sublanes:]):
                    states = [s * a + part for s, a in zip(states, steps)] if states else [part] * modes
            for n in range(modes):
                state = states[n]
                for at in range(3):
                    state = state + spread(over_ref, at * modes + n, cols) * pltpu.roll(state, 1 << at, 0)
                total_ref[pl.ds(n, 1), cols] = state[sublanes - 1 :]
            sent_ref[:, cols] = total_ref[:, cols].astype(jnp.bfloat16)

    for copy in side:
        copy.wait()


def local_kernel(
    piece, decay_ref, res_ref, skip_ref, sig_ref, v_ref, x_ref, base_ref, lead_ref, rows_ref, runs_ref, conv_ref
):
    modes = decay_ref.shape[0]
    span = sig_ref.shape[0] // sublanes
    run = lax.broadcasted_iota(jnp.int32, (sublanes, lanes), 0)
    ahead = (run + 1).astype(jnp.float32)

    def shifted(state, by):
        return jnp.where(run >= by, pltpu.roll(state, by, 0), 0.0)

    @pl.loop(0, piece_width // lanes)
    def _(group):
        here = at_group(group)
        cols = at_group(group + piece * (piece_width // lanes))
        rows_ref[...] = sig_ref[:, cols].astype(jnp.float32)
        for j in range(span):
            runs_ref[pl.ds(j * sublanes, sublanes), :] = rows_ref[pl.ds(j, sublanes, stride=span), :]
        skip = jnp.broadcast_to(skip_ref[:, cols], (sublanes, lanes))
        half = modes // 2
        for low in range(0, modes, half):
            decays = [spread(decay_ref, n, cols) for n in range(low, low + half)]
            gains = [spread(res_ref, n, cols) for n in range(low, low + half)]
            steps = [jnp.exp(-d) for d in decays]
            states = None
            for j in range(span):
                sig = runs_ref[pl.ds(j * sublanes, sublanes), :]
                states = [s * a + sig for s, a in zip(states, steps)] if j else [sig] * half
            for n in range(half):
                state = states[n]
                over = jnp.exp(decays[n] * float(-span))
                for by in (1, 2, 4):
                    state = state + over * shifted(state, by)
                    over = over * over
                states[n] = gains[n] * shifted(state, 1)
                lead_ref[low + n, :, here] = gains[n] * jnp.exp(-decays[n] * ahead)
            for j in range(span):
                sig = runs_ref[pl.ds(j * sublanes, sublanes), :]
                states = [s * a + sig * g for s, a, g in zip(states, steps, gains)]
                out = conv_ref.at[pl.ds(j, sublanes, stride=span), :]
                if low == 0:
                    out[...] = tree_sum(states) + skip * sig
                else:
                    out[...] = out[...] + tree_sum(states)
        mixed = v_ref[:, cols].astype(jnp.float32) * conv_ref[...]
        base_ref[:, here] = x_ref[:, cols].astype(jnp.float32) + mixed


def merge_kernel(size, rows, order, first, last, decay_ref, total_ref, *rest):
    position = lax.axis_index("ctx")
    odd = (position & size) != 0
    high = (position & (2 * size)) != 0
    decay = decay_ref[...]
    near, far, across = (rest[order.index(at)][...].astype(jnp.float32) for at in range(3))
    rest = rest[3:]
    over = jnp.exp(decay * float(-rows * size))
    other = jnp.where(odd, across * over + far, far * over + across)
    enter = jnp.where(high, jnp.where(odd, other * over, other), 0.0) + jnp.where(odd, near, 0.0)
    if not first:
        within = (position & (size - 1)).astype(jnp.float32) * float(rows)
        enter = rest[0][...] + enter * jnp.exp(decay * -within)
        rest = rest[1:]
    rest[0][...] = enter
    if not last:
        total = total_ref[...]
        own = jnp.where(odd, near * over + total, total * over + near)
        whole = jnp.where(high, other * (over * over) + own, own * (over * over) + other)
        rest[1][...] = whole.astype(jnp.bfloat16)
        rest[2][...] = whole


def finish_kernel(enter_ref, tile_ref, v_ref, *rest):
    pieces = (len(rest) - 3) // 2
    base_refs, lead_refs = rest[:pieces], rest[pieces:-3]
    new_ref, power_ref, acc_ref = rest[-3:]
    modes = tile_ref.shape[0]
    rows = v_ref.shape[0]
    acc_ref[...] = jnp.zeros_like(acc_ref)
    for piece, (base_ref, lead_ref) in enumerate(zip(base_refs, lead_refs)):

        @pl.loop(0, piece_width // lanes)
        def _(group):
            here = at_group(group)
            cols = at_group(group + piece * (piece_width // lanes))
            steps = [spread(tile_ref, n, cols) for n in range(modes)]
            states = [lead_ref[n, :, here] * spread(enter_ref, n, cols) for n in range(modes)]
            for pair in range(rows // (2 * sublanes)):
                halves = []
                for half in range(2):
                    halves.append(tree_sum(states))
                    if pair * 2 + half + 1 < rows // sublanes:
                        states = [s * a for s, a in zip(states, steps)]
                at = pl.ds(pair * 2 * sublanes, 2 * sublanes)
                carried = jnp.concatenate(halves, axis=0)
                fresh = base_ref[at, here] + v_ref[at, cols].astype(jnp.float32) * carried
                fresh = fresh.astype(jnp.bfloat16)
                new_ref[at, cols] = fresh
                fresh = fresh.astype(jnp.float32)
                acc_ref[at, :] += fresh * fresh

    ones = jnp.ones((2 * sublanes, lanes), jnp.bfloat16)
    rest = acc_ref[...]
    sums = jnp.zeros((2 * sublanes, rows), jnp.float32)
    for _ in range(3):
        head = rest.astype(jnp.bfloat16)
        rest = rest - head.astype(jnp.float32)
        sums += lax.dot_general(ones, head, (((1,), (1,)), ((), ())), preferred_element_type=jnp.float32)
    power_ref[...] = sums[0:1]


def norm_kernel(channels, mine_ref, other_ref, gain_ref, new_ref, out_hbm, inv_ref, out_ref, sem):
    rows, width = new_ref.shape
    power = (mine_ref[...] + other_ref[...]) * (1.0 / channels)
    inverse = lax.rsqrt(power + epsilon)
    inv_ref[...] = jnp.transpose(jnp.broadcast_to(inverse, (lanes, rows)))
    part = width // sem.shape[0]

    def written(p):
        cols = pl.ds(pl.multiple_of(p * part, part), part)
        return pltpu.make_async_copy(out_ref.at[:, cols], out_hbm.at[:, cols], sem.at[p])

    @pl.loop(0, sem.shape[0])
    def _(p):
        for group in range(part // lanes):
            cols = at_group(p * (part // lanes) + group)
            scaled = new_ref[:, cols].astype(jnp.float32) * inv_ref[...] * gain_ref[:, cols]
            out_ref[:, cols] = scaled.astype(jnp.bfloat16)
        written(p).start()

    @pl.loop(0, sem.shape[0])
    def _(p):
        written(p).wait()


def shards(queries, key_proj, values, residues, decay_rates, skip_weight, stream, norm_gain):
    rows, width = queries.shape
    modes = decay_rates.shape[0]
    params = pltpu.CompilerParams(vmem_limit_bytes=vmem_bytes)
    f32, bf16 = jnp.float32, jnp.bfloat16
    in_vmem = pl.BlockSpec(memory_space=pltpu.VMEM)
    anywhere = pl.BlockSpec(memory_space=pl.ANY)
    pieces = width // piece_width

    far = [queries, key_proj, values, stream, decay_rates, residues, skip_weight[None, :]]
    far = [pltpu.with_memory_space_constraint(a, pltpu.HBM) for a in far]
    outs = [
        ((modes, width), f32),
        ((modes, width), bf16),
        ((rows, width), bf16),
        ((rows, width), bf16),
        ((rows, width), bf16),
        ((modes, width), f32),
        ((modes, width), f32),
        ((1, width), f32),
        ((modes, width), f32),
    ]
    total, sent, signal, near_values, near_stream, decay, gains, skip, tile = pl.pallas_call(
        state_kernel,
        in_specs=[anywhere] * len(far),
        out_specs=[in_vmem] * len(outs),
        out_shape=[pltpu.VMEM(shape, dtype) for shape, dtype in outs],
        scratch_shapes=[
            pltpu.VMEM((rows, width), bf16),
            pltpu.VMEM((rows, width), bf16),
            pltpu.VMEM((3 * modes, width), f32),
            pltpu.SemaphoreType.DMA((2, pieces + 1)),
            pltpu.SemaphoreType.DMA((5,)),
        ],
        compiler_params=params,
        cost_estimate=pl.CostEstimate(flops=2 * modes * rows * width, bytes_accessed=4 * rows * width, transcendentals=0),
        name="states",
    )(*far)

    def local_piece(piece, decay):
        return pl.pallas_call(
            functools.partial(local_kernel, piece),
            in_specs=[in_vmem] * 6,
            out_specs=[in_vmem] * 2,
            out_shape=[pltpu.VMEM((rows, piece_width), f32), pltpu.VMEM((modes, sublanes, piece_width), f32)],
            scratch_shapes=[pltpu.VMEM((rows, lanes), f32)] * 3,
            compiler_params=params,
            cost_estimate=pl.CostEstimate(
                flops=6 * modes * rows * piece_width, bytes_accessed=12 * rows * piece_width, transcendentals=0
            ),
            name="local",
        )(decay, gains, skip, signal, near_values, near_stream)

    def link(partner_of):
        places = [(z, y, x) for z in range(8) for y in range(2) for x in range(4)]
        index = lambda z, y, x: (z * 2 + y) * 4 + x
        return [(index(*at), index(*partner_of(*at))) for at in places]

    stages = [
        [link(lambda z, y, x, k=k: (z, y, x ^ k)) for k in (1, 2, 3)],
        [link(lambda z, y, x, k=k: (z ^ (k >> 1), y ^ (k & 1), x)) for k in (1, 2, 3)],
        [link(lambda z, y, x, k=k: (z ^ k, y, x)) for k in (2, 5, 6)],
    ]

    def merge(size, order, last, total, arrived, enter):
        operands = [decay, total, *arrived] + ([] if enter is None else [enter])
        outs = [f32] if last else [f32, bf16, f32]
        return pl.pallas_call(
            functools.partial(merge_kernel, size, rows, order, enter is None, last),
            in_specs=[in_vmem] * len(operands),
            out_specs=[in_vmem] * len(outs),
            out_shape=[pltpu.VMEM((modes, width), dtype) for dtype in outs],
            compiler_params=params,
            name="merge",
        )(*operands)

    enter = None
    bases, leads = [], []
    for level, (links, beside) in enumerate(zip(stages, pieces_beside)):
        order = send_order[level]
        arrived = [lax.ppermute(sent, "ctx", links[at]) for at in order]
        tied, sent = lax.optimization_barrier((decay, sent))
        made = [local_piece(len(bases) + at, tied) for at in range(beside)]
        arrived, made = lax.optimization_barrier((arrived, made))
        bases += [base for base, _ in made]
        leads += [lead for _, lead in made]
        last = level + 1 == len(stages)
        merged = merge(4**level, order, last, total, arrived, enter)
        enter = merged[0]
        if not last:
            sent, total = merged[1:]

    fresh, power = pl.pallas_call(
        finish_kernel,
        in_specs=[in_vmem] * (3 + 2 * pieces),
        out_specs=[in_vmem] * 2,
        out_shape=[pltpu.VMEM((rows, width), bf16), pltpu.VMEM((1, rows), f32)],
        scratch_shapes=[pltpu.VMEM((rows, lanes), f32)],
        compiler_params=params,
        cost_estimate=pl.CostEstimate(flops=2 * modes * rows * width, bytes_accessed=8 * rows * width, transcendentals=0),
        name="finish",
    )(enter, tile, near_values, *bases, *leads)

    power = power + lax.ppermute(power, "tp", [(i, i ^ 1) for i in range(4)])
    other = lax.ppermute(power, "tp", [(i, i ^ 3) for i in range(4)])

    channels = width * lax.axis_size("tp")
    normed = pl.pallas_call(
        functools.partial(norm_kernel, channels),
        in_specs=[in_vmem] * 4,
        out_specs=anywhere,
        out_shape=pltpu.HBM((rows, width), bf16),
        scratch_shapes=[
            pltpu.VMEM((rows, lanes), f32),
            pltpu.VMEM((rows, width), bf16),
            pltpu.SemaphoreType.DMA((8,)),
        ],
        compiler_params=params,
        name="normalise",
    )(power, other, norm_gain[None, :], fresh)
    return (fresh, normed)


def solution(mesh):
    in_specs = (
        P("ctx", "tp"),
        P("ctx", "tp"),
        P("ctx", "tp"),
        P(None, "tp"),
        P(None, "tp"),
        P("tp"),
        P("ctx", "tp"),
        P("tp"),
    )
    out_specs = (P("ctx", "tp"), P("ctx", "tp"))
    return jax.shard_map(shards, mesh=mesh, in_specs=in_specs, out_specs=out_specs, check_vma=False)
```

```python
import functools

import jax
import jax.numpy as jnp
from jax import lax
from jax.experimental import pallas as pl
from jax.experimental.pallas import tpu as pltpu
from jax.sharding import PartitionSpec as P

epsilon = 1e-06
lanes = 128
sublanes = 8
piece_width = 256
pieces_beside = (2, 3, 3)
send_order = ((1, 2, 0), (2, 0, 1), (1, 2, 0))
vmem_bytes = 24 * 1024 * 1024


def at_group(group):
    return pl.ds(pl.multiple_of(group * lanes, lanes), lanes)


def spread(ref, mode, cols):
    return jnp.broadcast_to(ref[pl.ds(mode, 1), cols], (sublanes, lanes))


def tree_sum(parts):
    parts = list(parts)
    while len(parts) > 1:
        parts = [l + r for l, r in zip(parts[::2], parts[1::2])]
    return parts[0]


def state_kernel(
    q_hbm, k_hbm, v_hbm, x_hbm, decay_hbm, res_hbm, skip_hbm,
    total_ref, sent_ref, sig_ref, v_ref, x_ref, decay_ref, res_ref, skip_ref, tile_ref,
    q_ref, k_ref, over_ref, pair_sem, side_sem,
):
    modes = decay_ref.shape[0]
    rows, width = q_ref.shape
    edges = [0, 256, 1024, width]
    pair = []
    first = pltpu.make_async_copy(decay_hbm, decay_ref, side_sem.at[0])
    first.start()
    for p, (low, high) in enumerate(zip(edges, edges[1:])):
        cols = pl.ds(low, high - low)
        for at, (src, dst) in enumerate(((q_hbm, q_ref), (k_hbm, k_ref))):
            pair.append(pltpu.make_async_copy(src.at[:, cols], dst.at[:, cols], pair_sem.at[at, p]))
            pair[-1].start()
    side = []
    for at, (src, dst) in enumerate(((res_hbm, res_ref), (skip_hbm, skip_ref), (v_hbm, v_ref), (x_hbm, x_ref))):
        side.append(pltpu.make_async_copy(src, dst, side_sem.at[at + 1]))
        side[-1].start()
    first.wait()
    decay = decay_ref[...]
    tile_ref[...] = jnp.exp(decay * float(-sublanes))
    for at in range(3):
        over_ref[pl.ds(at * modes, modes), :] = jnp.exp(decay * float(-1 << at))
    for p, (low, high) in enumerate(zip(edges, edges[1:])):
        pair[2 * p].wait()
        pair[2 * p + 1].wait()

        @pl.loop(low // lanes, high // lanes, unroll=2)
        def _(group):
            cols = at_group(group)
            steps = [spread(tile_ref, n, cols) for n in range(modes)]
            states = None
            for j in range(0, rows, 2 * sublanes):
                at = pl.ds(j, 2 * sublanes)
                sig = q_ref[at, cols] * k_ref[at, cols]
                sig_ref[at, cols] = sig
                sig = sig.astype(jnp.float32)
                for part in (sig[:sublanes], sig[sublanes:]):
                    states = [s * a + part for s, a in zip(states, steps)] if states else [part] * modes
            for n in range(modes):
                state = states[n]
                for at in range(3):
                    state = state + spread(over_ref, at * modes + n, cols) * pltpu.roll(state, 1 << at, 0)
                total_ref[pl.ds(n, 1), cols] = state[sublanes - 1 :]
            sent_ref[:, cols] = total_ref[:, cols].astype(jnp.bfloat16)

    for copy in side:
        copy.wait()


def local_kernel(
    piece, decay_ref, res_ref, skip_ref, sig_ref, v_ref, x_ref, base_ref, lead_ref, rows_ref, runs_ref, conv_ref
):
    modes = decay_ref.shape[0]
    span = sig_ref.shape[0] // sublanes
    run = lax.broadcasted_iota(jnp.int32, (sublanes, lanes), 0)
    ahead = (run + 1).astype(jnp.float32)

    def shifted(state, by):
        return jnp.where(run >= by, pltpu.roll(state, by, 0), 0.0)

    @pl.loop(0, piece_width // lanes)
    def _(group):
        here = at_group(group)
        cols = at_group(group + piece * (piece_width // lanes))
        rows_ref[...] = sig_ref[:, cols].astype(jnp.float32)
        for j in range(span):
            runs_ref[pl.ds(j * sublanes, sublanes), :] = rows_ref[pl.ds(j, sublanes, stride=span), :]
        skip = jnp.broadcast_to(skip_ref[:, cols], (sublanes, lanes))
        half = modes // 2
        for low in range(0, modes, half):
            decays = [spread(decay_ref, n, cols) for n in range(low, low + half)]
            gains = [spread(res_ref, n, cols) for n in range(low, low + half)]
            steps = [jnp.exp(-d) for d in decays]
            states = None
            for j in range(span):
                sig = runs_ref[pl.ds(j * sublanes, sublanes), :]
                states = [s * a + sig for s, a in zip(states, steps)] if j else [sig] * half
            for n in range(half):
                state = states[n]
                over = jnp.exp(decays[n] * float(-span))
                for by in (1, 2, 4):
                    state = state + over * shifted(state, by)
                    over = over * over
                states[n] = gains[n] * shifted(state, 1)
                lead_ref[low + n, :, here] = gains[n] * jnp.exp(-decays[n] * ahead)
            for j in range(span):
                sig = runs_ref[pl.ds(j * sublanes, sublanes), :]
                states = [s * a + sig * g for s, a, g in zip(states, steps, gains)]
                out = conv_ref.at[pl.ds(j, sublanes, stride=span), :]
                if low == 0:
                    out[...] = tree_sum(states) + skip * sig
                else:
                    out[...] = out[...] + tree_sum(states)
        mixed = v_ref[:, cols].astype(jnp.float32) * conv_ref[...]
        base_ref[:, here] = x_ref[:, cols].astype(jnp.float32) + mixed


def merge_kernel(size, rows, order, first, last, decay_ref, total_ref, *rest):
    position = lax.axis_index("ctx")
    odd = (position & size) != 0
    high = (position & (2 * size)) != 0
    decay = decay_ref[...]
    near, far, across = (rest[order.index(at)][...].astype(jnp.float32) for at in range(3))
    rest = rest[3:]
    over = jnp.exp(decay * float(-rows * size))
    other = jnp.where(odd, across * over + far, far * over + across)
    enter = jnp.where(high, jnp.where(odd, other * over, other), 0.0) + jnp.where(odd, near, 0.0)
    if not first:
        within = (position & (size - 1)).astype(jnp.float32) * float(rows)
        enter = rest[0][...] + enter * jnp.exp(decay * -within)
        rest = rest[1:]
    rest[0][...] = enter
    if not last:
        total = total_ref[...]
        own = jnp.where(odd, near * over + total, total * over + near)
        whole = jnp.where(high, other * (over * over) + own, own * (over * over) + other)
        rest[1][...] = whole.astype(jnp.bfloat16)
        rest[2][...] = whole


def finish_kernel(size, order, decay_ref, one_ref, two_ref, three_ref, before_ref, tile_ref, v_ref, *rest):
    pieces = (len(rest) - 4) // 2
    base_refs, lead_refs = rest[:pieces], rest[pieces:-4]
    new_ref, power_ref, acc_ref, enter_ref = rest[-4:]
    modes = tile_ref.shape[0]
    rows = v_ref.shape[0]
    merge_kernel(
        size, rows, order, False, True, decay_ref, None, one_ref, two_ref, three_ref, before_ref, enter_ref
    )
    acc_ref[...] = jnp.zeros_like(acc_ref)
    for piece, (base_ref, lead_ref) in enumerate(zip(base_refs, lead_refs)):

        @pl.loop(0, piece_width // lanes)
        def _(group):
            here = at_group(group)
            cols = at_group(group + piece * (piece_width // lanes))
            steps = [spread(tile_ref, n, cols) for n in range(modes)]
            states = [lead_ref[n, :, here] * spread(enter_ref, n, cols) for n in range(modes)]
            for pair in range(rows // (2 * sublanes)):
                halves = []
                for half in range(2):
                    halves.append(tree_sum(states))
                    if pair * 2 + half + 1 < rows // sublanes:
                        states = [s * a for s, a in zip(states, steps)]
                at = pl.ds(pair * 2 * sublanes, 2 * sublanes)
                carried = jnp.concatenate(halves, axis=0)
                fresh = base_ref[at, here] + v_ref[at, cols].astype(jnp.float32) * carried
                fresh = fresh.astype(jnp.bfloat16)
                new_ref[at, cols] = fresh
                fresh = fresh.astype(jnp.float32)
                acc_ref[at, :] += fresh * fresh

    ones = jnp.ones((2 * sublanes, lanes), jnp.bfloat16)
    rest = acc_ref[...]
    sums = jnp.zeros((2 * sublanes, rows), jnp.float32)
    for _ in range(3):
        head = rest.astype(jnp.bfloat16)
        rest = rest - head.astype(jnp.float32)
        sums += lax.dot_general(ones, head, (((1,), (1,)), ((), ())), preferred_element_type=jnp.float32)
    power_ref[...] = sums[0:1]


def norm_kernel(channels, mine_ref, other_ref, gain_ref, new_ref, out_hbm, inv_ref, out_ref, sem):
    rows, width = new_ref.shape
    power = (mine_ref[...] + other_ref[...]) * (1.0 / channels)
    inverse = lax.rsqrt(power + epsilon)
    inv_ref[...] = jnp.transpose(jnp.broadcast_to(inverse, (lanes, rows)))
    part = width // sem.shape[0]

    def written(p):
        cols = pl.ds(pl.multiple_of(p * part, part), part)
        return pltpu.make_async_copy(out_ref.at[:, cols], out_hbm.at[:, cols], sem.at[p])

    @pl.loop(0, sem.shape[0])
    def _(p):
        for group in range(part // lanes):
            cols = at_group(p * (part // lanes) + group)
            scaled = new_ref[:, cols].astype(jnp.float32) * inv_ref[...] * gain_ref[:, cols]
            out_ref[:, cols] = scaled.astype(jnp.bfloat16)
        written(p).start()

    @pl.loop(0, sem.shape[0])
    def _(p):
        written(p).wait()


def shards(queries, key_proj, values, residues, decay_rates, skip_weight, stream, norm_gain):
    rows, width = queries.shape
    modes = decay_rates.shape[0]
    params = pltpu.CompilerParams(vmem_limit_bytes=vmem_bytes)
    f32, bf16 = jnp.float32, jnp.bfloat16
    in_vmem = pl.BlockSpec(memory_space=pltpu.VMEM)
    anywhere = pl.BlockSpec(memory_space=pl.ANY)
    pieces = width // piece_width

    far = [queries, key_proj, values, stream, decay_rates, residues, skip_weight[None, :]]
    far = [pltpu.with_memory_space_constraint(a, pltpu.HBM) for a in far]
    outs = [
        ((modes, width), f32),
        ((modes, width), bf16),
        ((rows, width), bf16),
        ((rows, width), bf16),
        ((rows, width), bf16),
        ((modes, width), f32),
        ((modes, width), f32),
        ((1, width), f32),
        ((modes, width), f32),
    ]
    total, sent, signal, near_values, near_stream, decay, gains, skip, tile = pl.pallas_call(
        state_kernel,
        in_specs=[anywhere] * len(far),
        out_specs=[in_vmem] * len(outs),
        out_shape=[pltpu.VMEM(shape, dtype) for shape, dtype in outs],
        scratch_shapes=[
            pltpu.VMEM((rows, width), bf16),
            pltpu.VMEM((rows, width), bf16),
            pltpu.VMEM((3 * modes, width), f32),
            pltpu.SemaphoreType.DMA((2, pieces + 1)),
            pltpu.SemaphoreType.DMA((5,)),
        ],
        compiler_params=params,
        cost_estimate=pl.CostEstimate(flops=2 * modes * rows * width, bytes_accessed=4 * rows * width, transcendentals=0),
        name="states",
    )(*far)

    def local_piece(piece, decay):
        return pl.pallas_call(
            functools.partial(local_kernel, piece),
            in_specs=[in_vmem] * 6,
            out_specs=[in_vmem] * 2,
            out_shape=[pltpu.VMEM((rows, piece_width), f32), pltpu.VMEM((modes, sublanes, piece_width), f32)],
            scratch_shapes=[pltpu.VMEM((rows, lanes), f32)] * 3,
            compiler_params=params,
            cost_estimate=pl.CostEstimate(
                flops=6 * modes * rows * piece_width, bytes_accessed=12 * rows * piece_width, transcendentals=0
            ),
            name="local",
        )(decay, gains, skip, signal, near_values, near_stream)

    def link(partner_of):
        places = [(z, y, x) for z in range(8) for y in range(2) for x in range(4)]
        index = lambda z, y, x: (z * 2 + y) * 4 + x
        return [(index(*at), index(*partner_of(*at))) for at in places]

    stages = [
        [link(lambda z, y, x, k=k: (z, y, x ^ k)) for k in (1, 2, 3)],
        [link(lambda z, y, x, k=k: (z ^ (k >> 1), y ^ (k & 1), x)) for k in (1, 2, 3)],
        [link(lambda z, y, x, k=k: (z ^ k, y, x)) for k in (2, 5, 6)],
    ]

    def merge(size, order, last, total, arrived, enter):
        operands = [decay, total, *arrived] + ([] if enter is None else [enter])
        outs = [f32] if last else [f32, bf16, f32]
        return pl.pallas_call(
            functools.partial(merge_kernel, size, rows, order, enter is None, last),
            in_specs=[in_vmem] * len(operands),
            out_specs=[in_vmem] * len(outs),
            out_shape=[pltpu.VMEM((modes, width), dtype) for dtype in outs],
            compiler_params=params,
            name="merge",
        )(*operands)

    enter = None
    bases, leads = [], []
    for level, (links, beside) in enumerate(zip(stages, pieces_beside)):
        order = send_order[level]
        arrived = [lax.ppermute(sent, "ctx", links[at]) for at in order]
        tied, sent = lax.optimization_barrier((decay, sent))
        made = [local_piece(len(bases) + at, tied) for at in range(beside)]
        arrived, made = lax.optimization_barrier((arrived, made))
        bases += [base for base, _ in made]
        leads += [lead for _, lead in made]
        last = level + 1 == len(stages)
        if not last:
            enter, sent, total = merge(4**level, order, last, total, arrived, enter)

    fresh, power = pl.pallas_call(
        functools.partial(finish_kernel, 4**level, order),
        in_specs=[in_vmem] * (7 + 2 * pieces),
        out_specs=[in_vmem] * 2,
        out_shape=[pltpu.VMEM((rows, width), bf16), pltpu.VMEM((1, rows), f32)],
        scratch_shapes=[pltpu.VMEM((rows, lanes), f32), pltpu.VMEM((modes, width), f32)],
        compiler_params=params,
        cost_estimate=pl.CostEstimate(flops=2 * modes * rows * width, bytes_accessed=8 * rows * width, transcendentals=0),
        name="finish",
    )(decay, *arrived, enter, tile, near_values, *bases, *leads)

    power = power + lax.ppermute(power, "tp", [(i, i ^ 1) for i in range(4)])
    other = lax.ppermute(power, "tp", [(i, i ^ 3) for i in range(4)])

    channels = width * lax.axis_size("tp")
    normed = pl.pallas_call(
        functools.partial(norm_kernel, channels),
        in_specs=[in_vmem] * 4,
        out_specs=anywhere,
        out_shape=pltpu.HBM((rows, width), bf16),
        scratch_shapes=[
            pltpu.VMEM((rows, lanes), f32),
            pltpu.VMEM((rows, width), bf16),
            pltpu.SemaphoreType.DMA((8,)),
        ],
        compiler_params=params,
        name="normalise",
    )(power, other, norm_gain[None, :], fresh)
    return (fresh, normed)


def solution(mesh):
    in_specs = (
        P("ctx", "tp"),
        P("ctx", "tp"),
        P("ctx", "tp"),
        P(None, "tp"),
        P(None, "tp"),
        P("tp"),
        P("ctx", "tp"),
        P("tp"),
    )
    out_specs = (P("ctx", "tp"), P("ctx", "tp"))
    return jax.shard_map(shards, mesh=mesh, in_specs=in_specs, out_specs=out_specs, check_vma=False)
```
